32 devices in a mesh: freq: 2 (over x), sub: 16 (over z, y, core).
Axes of the slice: x: 2, y: 2, z: 4, core: 2. Of those that a mesh axis runs over, the one named last changes fastest.
Arguments:
- forward_base: float32 [2, 2, 128, 256, 128], P('freq', None, 'sub'), may hold values from -6 to 6
- source: float32 [2, 2, 128, 256, 128], P('freq', None, 'sub'), may hold values from -6 to 6
- slowness_sq: float32 [128, 256, 128], P('sub'), may hold values from 0.25 to 2
- receiver_rows: bfloat16 [2, 4096, 256], P('freq', 'sub'), may hold values from -6 to 6
- rec_owner: int32 [4096, 1], P('sub'), may hold values from 0 to 15; in each aligned block of 256 rows (0 to 255, 256 to 511, ...) at most 32 rows name the same one
- rec_cell: int32 [4096], P('sub'), may hold values from 0 to 2047
- sep_rhs: float32 [2, 3, 2, 32768], P('freq', None, None, 'sub'), may hold values from -6 to 6
- sep_diag: float32 [2, 3, 32768], P('freq', None, 'sub'), may hold values from 0.5 to 2
- gen_u: float32 [2, 3, 2, 32768, 256], P('freq', None, None, 'sub'), may hold values from -0.25 to 0.25
- gen_v: float32 [2, 3, 2, 32768, 256], P('freq', None, None, 'sub'), may hold values from -0.0234375 to 0.0234375
- gen_w: float32 [2, 3, 2, 256, 256], P('freq'), may hold values from -0.25 to 0.25
Outputs:
- gradient: float32 [128, 256, 128], P('sub')
The draws below stay inside these ranges and needn't reach their ends.
Inputs may be any that keep to these rules, and one draw needn't show every extreme that they name: `rec_owner`: among the 256 receiver lines of one index of sub, at most 32 name the same owner, a bound that some block reaches of them.
All inputs are finite; a program needn't handle non-finite values.
Results may differ from the reference program's by a relative error of at most 0.005.
Values may be sent and summed in bfloat16 or wider, within the bound.
A program may use at most 128 MiB of HBM per device.

```python
import math
import jax
import jax.numpy as jnp
import numpy as np
from jax import lax

CX = 8
NY = 256
NZ = 128
R = 256
FRONTS = 3
REC_DEV = 256
FREQS = 2
NX = 128
PLANE = 32768
CAP = 32
RECEIVERS = 4096
N_SUB = 16


def with_ends(result, key, least, largest):
    dims = result.shape
    spot = [jax.random.randint(jax.random.fold_in(key, axis), (), 0, dims[axis]) for axis in range(len(dims))]
    result = result.at[tuple(spot)].set(least)
    longest = dims.index(max(dims))
    spot[longest] = (spot[longest] + 1) % dims[longest]
    return result.at[tuple(spot)].set(largest)


def shard_levels(rng, shape, split, least, top_value):
    def one(position, shards_of):
        heights = jax.random.uniform(jax.random.fold_in(jax.random.fold_in(rng, 6), position), (shards_of,), jnp.float32, least / len(split), top_value / len(split))
        return jnp.repeat(jnp.exp(heights), shape[position] // shards_of).reshape((-1,) + (1,) * (len(shape) - position - 1))

    factor_of = one(*split[0])
    for cut in split[1:]:
        factor_of = factor_of * one(*cut)
    return factor_of


def assign_block(stream_key, own, number, rows, amount, top, most, skew):
    order = jax.random.permutation(stream_key, amount)
    crowded, ordinary = shares(amount, rows * top, most, skew, True), shares(amount, rows * top, most, skew, False)
    places = jnp.arange(amount)

    def named(sizes, offset_by):
        used = int((sizes > 0).sum())
        fixed = max(1, used // 4)
        moved = fixed + (places - fixed + offset_by * (used - fixed)) % max(1, amount - fixed)
        return jnp.zeros((amount,), jnp.int32).at[order[jnp.where(places < fixed, places, moved)]].set(jnp.asarray(sizes, jnp.int32))

    sizes = jnp.where(number % 4 == 0, named(crowded, number // 4), named(ordinary, number - number // 4 - 1))
    mixed = jax.random.permutation(jax.random.fold_in(own, 3), amount)
    giver, receiver = mixed[0:amount // 2 * 2:2], mixed[1:amount // 2 * 2:2]
    room = jnp.minimum(sizes[giver] - 1, most - sizes[receiver]) // 2
    room = jnp.where((giver == order[0]) | (receiver == order[0]) | (sizes[receiver] == 0), 0, jnp.maximum(room, 0))
    moved = jax.random.randint(jax.random.fold_in(own, 4), (amount // 2,), 0, 1 << 20) % (room + 1)
    sizes = sizes.at[giver].add(-moved).at[receiver].add(moved)
    labels = jnp.searchsorted(jnp.cumsum(sizes), jnp.arange(rows * top), side="right").astype(jnp.int32)
    listing = labels.reshape(top, rows).T
    listing = listing[jax.random.permutation(jax.random.fold_in(own, 1), rows)]
    offset_by = jax.random.randint(jax.random.fold_in(own, 2), (rows, 1), 0, top)
    return jnp.take_along_axis(listing, (jnp.arange(top)[None, :] + offset_by) % top, axis=1)


def shares(number_of, total, bound, skew, full):
    loads = [(1 << 20) // math.isqrt(standing ** skew) + 1 for standing in range(1, number_of + 1)]
    largest = bound if full else min(bound, max(-(-total // number_of), total * loads[0] // sum(loads)))
    least = 1 if total - largest >= number_of - 1 else 0
    counts, rest = [largest] + [least] * (number_of - 1), total - largest - least * (number_of - 1)
    while rest > 0:
        free = [i for i in range(1, number_of) if counts[i] < largest] or [i for i in range(1, number_of) if counts[i] < bound]
        mass, budget = sum([loads[i] for i in free]), rest
        for i in free:
            addition = min(bound - counts[i], max(1, budget * loads[i] // mass), rest)
            counts[i] = counts[i] + addition
            rest = rest - addition
    return np.array(counts)


def normal_values(key, dims, scale, bound, split=(), held_as=jnp.bfloat16):
    values = scale * jax.random.normal(key, dims, jnp.float32)
    if split:
        values = values * shard_levels(key, dims, split, -0.22, 0.18)
    return jnp.clip(values, -bound, bound).astype(held_as)


def setup_inputs(seed: int = 0) -> dict:
    splits = jax.random.split(jax.random.key(seed), 12)
    forward_base = normal_values(splits[0], (FREQS, 2, NX, NY, NZ), 1.0, 6.0, ((0, 2), (2, 16)), jnp.float32)
    source = normal_values(splits[1], (FREQS, 2, NX, NY, NZ), 1.0, 6.0, ((0, 2), (2, 16)), jnp.float32)
    slowness_sq = jnp.clip(jnp.exp(math.log(2.0) - 2.0794415 * jax.random.uniform(splits[2], (NX, NY, NZ), jnp.float32) ** shard_levels(splits[2], (NX, NY, NZ), ((0, 16),), -0.2, 0.2)), 0.25, 2.0)
    receiver_rows = normal_values(splits[3], (FREQS, RECEIVERS, 2 * NZ), 1.0, 6.0, ((0, 2), (1, 16)))
    rec_owner_keys = jax.random.split(jax.random.fold_in(splits[4], 1), RECEIVERS // REC_DEV)
    rec_owner_turns = jax.random.permutation(jax.random.fold_in(splits[4], 3), RECEIVERS // REC_DEV)
    rec_owner = jax.vmap(lambda own, number: assign_block(jax.random.fold_in(splits[4], 2), own, number, REC_DEV, N_SUB, 1, CAP, 2))(rec_owner_keys, rec_owner_turns).reshape((RECEIVERS, 1))
    rec_cell = with_ends(jax.random.randint(splits[5], (RECEIVERS,), 0, CX * NY), jax.random.fold_in(splits[5], 1), 0, (CX * NY) - 1).astype(jnp.int32)
    sep_rhs = normal_values(splits[6], (FREQS, FRONTS, 2, PLANE), 1.0, 6.0, ((0, 2), (3, 16)), jnp.float32)
    sep_diag = jnp.clip(jnp.exp(math.log(2.0) - 1.3862944 * jax.random.uniform(splits[7], (FREQS, FRONTS, PLANE), jnp.float32) ** shard_levels(splits[7], (FREQS, FRONTS, PLANE), ((0, 2), (2, 16)), -0.2, 0.2)), 0.5, 2.0)
    gen_u = normal_values(splits[8], (FREQS, FRONTS, 2, PLANE, R), (2 * R) ** -0.5, 0.25, ((0, 2), (3, 16)), jnp.float32)
    gen_v = normal_values(splits[9], (FREQS, FRONTS, 2, PLANE, R), (2 * PLANE) ** -0.5, 0.0234375, ((0, 2), (3, 16)), jnp.float32)
    gen_w = normal_values(splits[10], (FREQS, FRONTS, 2, R, R), (2 * R) ** -0.5, 0.25, ((0, 2),), jnp.float32)
    return dict(forward_base=forward_base, source=source, slowness_sq=slowness_sq, receiver_rows=receiver_rows, rec_owner=rec_owner, rec_cell=rec_cell, sep_rhs=sep_rhs, sep_diag=sep_diag, gen_u=gen_u, gen_v=gen_v, gen_w=gen_w)


reach_weights = (0.6, 0.15, 0.05)


def stencil_apply(padded, center):
    layers = center.shape[2]
    row_count = center.shape[3]
    depth_count = center.shape[4]
    accumulated = [jnp.zeros_like(center), jnp.zeros_like(center), jnp.zeros_like(center)]
    for step_x in range(3):
        for step_y in range(3):
            for step_z in range(3):
                reach_len = abs(step_x - 1) + abs(step_y - 1) + abs(step_z - 1)
                if reach_len > 0:
                    shifted = padded[:, :, step_x:step_x + layers, step_y:step_y + row_count, step_z:step_z + depth_count]
                    accumulated[reach_len - 1] = accumulated[reach_len - 1] + shifted
    combined = reach_weights[0] * accumulated[0] + reach_weights[1] * accumulated[1] + reach_weights[2] * accumulated[2]
    return combined - 5.8 * center


def front_correction(values, first_layer, layer_count, grid_x, row_count, depth_count):
    planes = values.reshape(values.shape[0], values.shape[1], 2, row_count, depth_count)
    positions = (grid_x // 2, grid_x // 4, 3 * grid_x // 4)
    decay_len = grid_x / 4.0
    layer_ids = (first_layer + jnp.arange(layer_count)).astype(jnp.float32)
    inside = (layer_ids >= 0.0) & (layer_ids < float(grid_x))
    summed = None
    for front in range(3):
        decay_coef = jnp.where(inside, jnp.exp(-jnp.abs(layer_ids - float(positions[front])) / decay_len), 0.0)
        front_term = decay_coef[None, None, :, None, None] * planes[:, front][:, :, None]
        summed = front_term if summed is None else summed + front_term
    return summed


def reference(forward_base, source, slowness_sq, receiver_rows, rec_owner, rec_cell, sep_rhs, sep_diag, gen_u, gen_v, gen_w):
    highest = lax.Precision.HIGHEST
    rhs_re = sep_rhs[:, :, 0]
    rhs_im = sep_rhs[:, :, 1]
    proj_re = jnp.einsum("fkpr,fkp->fkr", gen_v[:, :, 0], rhs_re, precision=highest) - jnp.einsum("fkpr,fkp->fkr", gen_v[:, :, 1], rhs_im, precision=highest)
    proj_im = jnp.einsum("fkpr,fkp->fkr", gen_v[:, :, 0], rhs_im, precision=highest) + jnp.einsum("fkpr,fkp->fkr", gen_v[:, :, 1], rhs_re, precision=highest)
    mixed_re = jnp.einsum("fkst,fkt->fks", gen_w[:, :, 0], proj_re, precision=highest) - jnp.einsum("fkst,fkt->fks", gen_w[:, :, 1], proj_im, precision=highest)
    mixed_im = jnp.einsum("fkst,fkt->fks", gen_w[:, :, 0], proj_im, precision=highest) + jnp.einsum("fkst,fkt->fks", gen_w[:, :, 1], proj_re, precision=highest)
    value_re = sep_diag * rhs_re + (jnp.einsum("fkpr,fkr->fkp", gen_u[:, :, 0], mixed_re, precision=highest) - jnp.einsum("fkpr,fkr->fkp", gen_u[:, :, 1], mixed_im, precision=highest))
    value_im = sep_diag * rhs_im + (jnp.einsum("fkpr,fkr->fkp", gen_u[:, :, 0], mixed_im, precision=highest) + jnp.einsum("fkpr,fkr->fkp", gen_u[:, :, 1], mixed_re, precision=highest))
    values = jnp.stack([value_re, value_im], axis=2)
    wavefield = forward_base + front_correction(values, 0, NX, NX, NY, NZ)
    padded = jnp.pad(wavefield, ((0, 0), (0, 0), (1, 1), (1, 1), (1, 1)))
    angular = (1.0 + 0.5 * jnp.arange(FREQS).astype(jnp.float32)).reshape(FREQS, 1, 1, 1, 1)
    residual_field = angular ** 2 * slowness_sq[None, None] * wavefield + stencil_apply(padded, wavefield) - source
    owners = rec_owner[:, 0]
    segment_ids = owners * (CX * NY) + rec_cell
    line_rows = jnp.transpose(receiver_rows.astype(jnp.float32), (1, 0, 2)).reshape(RECEIVERS, FREQS * 2 * NZ)
    injected = jax.ops.segment_sum(line_rows, segment_ids, num_segments=NX * NY)
    injected = jnp.transpose(injected.reshape(NX, NY, FREQS, 2, NZ), (2, 3, 0, 1, 4))
    adjoint = residual_field + injected
    return jnp.sum(angular[:, 0] ** 2 * (wavefield[:, 0] * adjoint[:, 0] + wavefield[:, 1] * adjoint[:, 1]), axis=0)
```

```python
import functools

import jax
import jax.numpy as jnp
from jax import lax
from jax.experimental import pallas as pl
from jax.experimental.pallas import tpu as pltpu
from jax.sharding import PartitionSpec as P

MESH = pl.DeviceIdType.MESH
F32, BF16, I16, I32 = jnp.float32, jnp.bfloat16, jnp.int16, jnp.int32
LOG2E, LN2, STEPS = 1.4426950408889634, 0.6931471805599453, 32760.0
NT = (((1,), (1,)), ((), ()))
NN = (((1,), (0,)), ((), ()))


def split_rows(pair):
    high = pair.astype(BF16).astype(F32)
    return jnp.concatenate([high, pair - high, jnp.zeros((4, pair.shape[1]), F32)], 0).astype(BF16)


def split_dot(left, right, dims):
    high = right.astype(BF16)
    low = (right - high.astype(F32)).astype(BF16)
    a = lax.dot_general(left, high, dims, preferred_element_type=F32)
    b = lax.dot_general(left, low, dims, preferred_element_type=F32)
    return a[0:2] + a[2:4] + b[0:2]


def scale_power(x):
    top = jnp.maximum(jnp.max(jnp.abs(x), axis=0, keepdims=True), 1e-30)
    return jnp.ceil(jnp.log(top) * LOG2E + 0.001)


def step_of(power):
    return jnp.exp(power * LN2) * (1.0 / STEPS)


def coded(x, power):
    return jnp.clip(jnp.round(x / step_of(power)), -32767.0, 32767.0)


def in_plane(x):
    rows, lanes = x.shape
    lane = lax.broadcasted_iota(I32, x.shape, 1)
    row = lax.broadcasted_iota(I32, x.shape, 0)

    def along_y(v):
        return jnp.where(row == 0, 0.0, pltpu.roll(v, 1, 0)) + jnp.where(
            row == rows - 1, 0.0, pltpu.roll(v, rows - 1, 0)
        )

    zs = jnp.where(lane == 0, 0.0, pltpu.roll(x, 1, 1)) + jnp.where(
        lane == lanes - 1, 0.0, pltpu.roll(x, lanes - 1, 1)
    )
    face = zs + along_y(x)
    diagonal = along_y(zs)
    inner = 0.6 * face + 0.15 * diagonal - 5.8 * x
    outer = 0.6 * x + 0.15 * face + 0.05 * diagonal
    return inner, outer


def kernel(
    n, cap,
    base_h, src_h, slow_h, u_h, v_h, w_h, rows_ref, ownc_ref, ownr_ref, cell_ref, rhs_ref, diag_ref,
    out_h,
    base, src, slow, u_buf, v_buf, w_buf, halo, g, planes, inner, outer, out_v,
    sum_buf, vals, pmsg, rt_send, rt_recv, gsend, grecv,
    in_sem, v_sem, u_sem, out_sem,
    halo_ss, halo_rs, rt_ss, rt_rs, sum_ss, sum_rs, pl_ss, pl_rs, gr_ss, gr_rs,
):
    me = lax.axis_index("sub")
    freq = lax.axis_index("freq")
    layers, ny, nz = base.shape[1:]
    fronts, _, prow, rank = u_buf.shape
    lines = rows_ref.shape[0]
    seg = prow // nz
    omega = 1.0 + 0.5 * freq.astype(F32)
    om2 = omega * omega

    def v_copy(k, c):
        return pltpu.make_async_copy(v_h.at[k, c], v_buf.at[k, c], v_sem.at[k, c])

    def u_copy(k, c):
        return pltpu.make_async_copy(u_h.at[k, c], u_buf.at[k, c], u_sem.at[k, c])

    pairs = [(k, c) for k in range(fronts) for c in range(2)]
    for k, c in pairs:
        v_copy(k, c).start()
    loads = [
        pltpu.make_async_copy(a, b, in_sem.at[i])
        for i, (a, b) in enumerate([(w_h, w_buf), (base_h, base), (src_h, src), (slow_h, slow)])
    ]
    for one in loads:
        one.start()
    for k, c in pairs:
        u_copy(k, c).start()

    barrier = pltpu.get_barrier_semaphore()

    @pl.loop(1, n)
    def _(i):
        pl.semaphore_signal(barrier, inc=1, device_id={"sub": lax.rem(me + i, n)}, device_id_type=MESH)

    pl.semaphore_signal(barrier, inc=1, device_id={"freq": 1 - freq}, device_id_type=MESH)
    pl.semaphore_wait(barrier, n)

    def remote(src_ref, dst_ref, ss, rs, dev):
        return pltpu.make_async_remote_copy(
            src_ref=src_ref, dst_ref=dst_ref, send_sem=ss, recv_sem=rs, device_id=dev, device_id_type=MESH
        )

    up = remote(base_h.at[:, layers - 1], halo.at[0], halo_ss.at[0], halo_rs.at[0], {"sub": me + 1})
    down = remote(base_h.at[:, 0], halo.at[1], halo_ss.at[1], halo_rs.at[1], {"sub": me - 1})

    @pl.when(me < n - 1)
    def _():
        up.start()

    @pl.when(me > 0)
    def _():
        down.start()

    own_row = ownr_ref[...]
    before = lax.broadcasted_iota(I32, (lines, lines), 0) < lax.broadcasted_iota(I32, (lines, lines), 1)
    same = (ownc_ref[...] == own_row) & before
    order = jnp.sum(jnp.where(same, 1.0, 0.0), axis=0, keepdims=True).astype(I32)
    slot = own_row * cap + order
    total = n * cap
    chosen = slot == lax.broadcasted_iota(I32, (total, lines), 0)
    picked = lax.dot_general(
        jnp.where(chosen, 1.0, 0.0).astype(BF16), rows_ref[...], NN, preferred_element_type=F32
    )
    rt_send[:, 0 : 2 * nz] = picked.astype(BF16)
    code = jnp.sum(jnp.where(chosen, (cell_ref[...] + 1).astype(F32), 0.0), axis=1, keepdims=True)
    high = jnp.floor(code * (1.0 / 64.0))
    lane = lax.broadcasted_iota(I32, (total, 128), 1)
    rt_send[:, 2 * nz : 2 * nz + 128] = jnp.where(lane < 64, high, code - 64.0 * high).astype(BF16)

    def at(i, size):
        return pl.ds(pl.multiple_of(i * size, size), size)

    def rt_copy(to, sender):
        return remote(
            rt_send.at[at(to, cap)], rt_recv.at[at(sender, cap)], rt_ss.at[to], rt_rs.at[sender], {"sub": to}
        )

    def sum_copy(to, sender):
        return remote(sum_buf.at[sender], sum_buf.at[sender], sum_ss.at[to], sum_rs.at[sender], {"sub": to})

    def pl_copy(to, sender):
        return remote(pmsg.at[sender], pmsg.at[sender], pl_ss.at[to], pl_rs.at[sender], {"sub": to})

    def start_all(make):
        @pl.loop(1, n)
        def _(i):
            make(lax.rem(me + i, n), me).start()

    def wait_all(make):
        @pl.loop(1, n)
        def _(i):
            make(me, lax.rem(me + n - i, n)).wait_recv()

    def sent_all(make):
        @pl.loop(1, n)
        def _(i):
            make(lax.rem(me + i, n), me).wait_send()

    start_all(rt_copy)
    rt_recv[at(me, cap), :] = rt_send[at(me, cap), :]

    tile = min(512, prow)
    for k in range(fronts):
        acc = []
        for c in range(2):
            v_copy(k, c).wait()

            def add(t, total_so_far, k=k, c=c):
                left = split_rows(rhs_ref[k, :, at(t, tile)])
                return total_so_far + split_dot(left, v_buf[k, c, at(t, tile), :], NN)

            acc.append(lax.fori_loop(0, prow // tile, add, jnp.zeros((2, rank), F32)))
        sum_buf[me, 2 * k : 2 * k + 1, :] = acc[0][0:1] - acc[1][1:2]
        sum_buf[me, 2 * k + 1 : 2 * k + 2, :] = acc[0][1:2] + acc[1][0:1]
    sum_buf[me, 2 * fronts : 8, :] = jnp.zeros((8 - 2 * fronts, rank), F32)
    start_all(sum_copy)

    for one in loads:
        one.wait()
    wait_all(rt_copy)
    marks = jnp.transpose(rt_recv[:, 2 * nz : 2 * nz + 128].astype(F32))
    place = 64.0 * marks[0:1] + marks[64:65]

    @pl.loop(0, layers)
    def _(x):
        first = (x * ny + 1).astype(F32)
        want = first + lax.broadcasted_iota(I32, (ny, total), 0).astype(F32)
        hot = jnp.where(place == want, 1.0, 0.0).astype(BF16)
        injected = lax.dot_general(hot, rt_recv[:, 0 : 2 * nz], NN, preferred_element_type=F32)
        for c in range(2):
            g[c, x + 1] = injected[:, c * nz : (c + 1) * nz] - src[c, x] + om2 * slow[x] * base[c, x]

    for c in range(2):
        g[c, 0] = jnp.zeros((ny, nz), F32)
        g[c, layers + 1] = jnp.zeros((ny, nz), F32)

    wait_all(sum_copy)
    proj = lax.fori_loop(0, n, lambda i, s: s + sum_buf[i], jnp.zeros((8, rank), F32))
    for k in range(fronts):
        left = split_rows(proj[2 * k : 2 * k + 2])
        wr = split_dot(left, w_buf[k, 0], NT)
        wi = split_dot(left, w_buf[k, 1], NT)
        mixed = split_rows(jnp.concatenate([wr[0:1] - wi[1:2], wr[1:2] + wi[0:1]], 0))
        u_copy(k, 0).wait()
        u_copy(k, 1).wait()

        @pl.loop(0, prow // tile)
        def _(t):
            ur = split_dot(mixed, u_buf[k, 0, at(t, tile), :], NT)
            ui = split_dot(mixed, u_buf[k, 1, at(t, tile), :], NT)
            own = diag_ref[k : k + 1, at(t, tile)] * rhs_ref[k, :, at(t, tile)]
            re = own[0:1] + (ur[0:1] - ui[1:2])
            im = own[1:2] + (ur[1:2] + ui[0:1])
            for j in range(tile // nz):
                vals[2 * k, pl.ds(t * (tile // nz) + j, 1), :] = re[:, j * nz : (j + 1) * nz]
                vals[2 * k + 1, pl.ds(t * (tile // nz) + j, 1), :] = im[:, j * nz : (j + 1) * nz]

    count = pmsg.shape[1]
    pieces, powers = [], []
    for q in range(2 * fronts):
        value = vals[q]
        power = scale_power(value)
        pieces.append(coded(value, power))
        powers.append(power)
    rest = count - 2 * fronts * (seg + 1)
    pieces = pieces + powers + ([jnp.zeros((rest, nz), F32)] if rest else [])
    pmsg[me] = jnp.concatenate(pieces, 0).astype(I32).astype(I16)
    start_all(pl_copy)

    @pl.loop(0, layers)
    def _(x):
        for c in range(2):
            a, b = in_plane(base[c, x])
            g[c, x + 1] += a
            g[c, x] += b
            g[c, x + 2] += b

    @pl.when(me > 0)
    def _():
        up.wait_recv()
        for c in range(2):
            g[c, 1] += in_plane(halo[0, c])[1]

    @pl.when(me < n - 1)
    def _():
        down.wait_recv()
        for c in range(2):
            g[c, layers] += in_plane(halo[1, c])[1]

    wait_all(pl_copy)

    @pl.loop(0, n)
    def _(i):
        got = pmsg[i].astype(I32).astype(F32)
        for q in range(2 * fronts):
            step = step_of(got[2 * fronts * seg + q : 2 * fronts * seg + q + 1])
            planes[q, pl.ds(i * seg, seg), :] = got[q * seg : (q + 1) * seg] * step

    @pl.loop(0, 2 * fronts)
    def _(q):
        a, b = in_plane(planes[q])
        inner[q] = a
        outer[q] = b

    grid = n * layers
    spots = (grid // 2, grid // 4, 3 * grid // 4)
    flat = jnp.zeros((1, nz), F32)

    def decay(where_x, spot):
        far = jnp.exp(flat - jnp.abs(where_x - spot).astype(F32) / (grid / 4.0))
        return jnp.where((flat.astype(I32) + where_x >= 0) & (flat.astype(I32) + where_x < grid), far, 0.0)

    def gr_copy(x):
        return remote(gsend.at[x], grecv.at[x], gr_ss.at[x], gr_rs.at[x], {"freq": 1 - freq})

    @pl.loop(0, layers)
    def _(x):
        layer = me * layers + x
        here = [decay(layer, s) for s in spots]
        beside = [decay(layer - 1, s) + decay(layer + 1, s) for s in spots]
        slowness = om2 * slow[x]
        grad = None
        for c in range(2):
            front = here[0] * planes[c]
            rest_of = g[c, x + 1]
            for k in range(fronts):
                q = 2 * k + c
                if k:
                    front = front + here[k] * planes[q]
                rest_of = rest_of + here[k] * inner[q] + beside[k] * outer[q]
            term = (base[c, x] + front) * (rest_of + slowness * front)
            grad = term if grad is None else grad + term
        grad = om2 * grad
        power = scale_power(grad)
        gsend[x, 0:ny, :] = coded(grad, power).astype(I32).astype(I16)
        gsend[x, ny : ny + 16, :] = jnp.broadcast_to(power, (16, nz)).astype(I32).astype(I16)
        gr_copy(x).start()

    def decoded(ref, x):
        step = step_of(ref[x, ny : ny + 16, :].astype(I32).astype(F32)[0:1])
        return ref[x, 0:ny, :].astype(I32).astype(F32) * step

    def out_copy(x):
        return pltpu.make_async_copy(out_v.at[x], out_h.at[x], out_sem.at[x])

    @pl.loop(0, layers)
    def _(x):
        gr_copy(x).wait_recv()
        out_v[x] = decoded(gsend, x) + decoded(grecv, x)
        out_copy(x).start()

    sent_all(rt_copy)
    sent_all(sum_copy)
    sent_all(pl_copy)

    @pl.when(me < n - 1)
    def _():
        up.wait_send()

    @pl.when(me > 0)
    def _():
        down.wait_send()

    @pl.loop(0, layers)
    def _(x):
        gr_copy(x).wait_send()
        out_copy(x).wait()


def body(n, base, src, slow, rows, owner, cell, rhs, diag, gu, gv, gw):
    layers, ny, nz = slow.shape
    fronts, _, prow, rank = gu.shape[1:]
    lines = cell.shape[0]
    cap = max(16, -(-max(2, 2 * lines // n) // 16) * 16)
    total = n * cap
    seg = prow // nz
    count = -(-(2 * fronts * (seg + 1)) // 16) * 16
    dma = pltpu.SemaphoreType.DMA
    hbm, vmem = pl.BlockSpec(memory_space=pl.ANY), pl.BlockSpec(memory_space=pltpu.VMEM)
    return pl.pallas_call(
        functools.partial(kernel, n, cap),
        out_shape=jax.ShapeDtypeStruct(slow.shape, F32),
        in_specs=[hbm] * 6 + [vmem] * 6,
        out_specs=hbm,
        scratch_shapes=[
            pltpu.VMEM((2, layers, ny, nz), F32),
            pltpu.VMEM((2, layers, ny, nz), F32),
            pltpu.VMEM((layers, ny, nz), F32),
            pltpu.VMEM((fronts, 2, prow, rank), F32),
            pltpu.VMEM((fronts, 2, prow, rank), F32),
            pltpu.VMEM((fronts, 2, rank, rank), F32),
            pltpu.VMEM((2, 2, ny, nz), F32),
            pltpu.VMEM((2, layers + 2, ny, nz), F32),
            pltpu.VMEM((2 * fronts, ny, nz), F32),
            pltpu.VMEM((2 * fronts, ny, nz), F32),
            pltpu.VMEM((2 * fronts, ny, nz), F32),
            pltpu.VMEM((layers, ny, nz), F32),
            pltpu.VMEM((n, 8, rank), F32),
            pltpu.VMEM((2 * fronts, seg, nz), F32),
            pltpu.VMEM((n, count, nz), I16),
            pltpu.VMEM((total, 2 * nz + 128), BF16),
            pltpu.VMEM((total, 2 * nz + 128), BF16),
            pltpu.VMEM((layers, ny + 16, nz), I16),
            pltpu.VMEM((layers, ny + 16, nz), I16),
            dma((4,)), dma((fronts, 2)), dma((fronts, 2)), dma((layers,)),
            dma((2,)), dma((2,)), dma((n,)), dma((n,)), dma((n,)), dma((n,)), dma((n,)), dma((n,)),
            dma((layers,)), dma((layers,)),
        ],
        compiler_params=pltpu.CompilerParams(
            collective_id=0, has_side_effects=True, vmem_limit_bytes=52 * 2**20
        ),
    )(
        base[0], src[0], slow, gu[0], gv[0], gw[0], rows[0], owner, owner.reshape(1, lines),
        cell.reshape(1, lines), rhs[0], diag[0],
    )


def solution(mesh):
    return jax.shard_map(
        functools.partial(body, mesh.shape["sub"]),
        mesh=mesh,
        in_specs=(
            P("freq", None, "sub", None, None),
            P("freq", None, "sub", None, None),
            P("sub", None, None),
            P("freq", "sub", None),
            P("sub", None),
            P("sub"),
            P("freq", None, None, "sub"),
            P("freq", None, "sub"),
            P("freq", None, None, "sub", None),
            P("freq", None, None, "sub", None),
            P("freq", None, None, None, None),
        ),
        out_specs=P("sub", None, None),
        check_vma=False,
    )
```
